256 devices in a mesh: expert: 8 (over z_hi, x), row: 32 (over y, z_lo, core).
Axes of the slice: x: 4, y: 4, z: 8 (z_hi: 2, z_lo: 4; z = z_hi * 4 + z_lo), core: 2. Of those that a mesh axis runs over, the one named last changes fastest.
Arguments:
- momentum: bfloat16 [256, 2048, 768], P('expert', 'row'), may hold values from -6 to 6
- gradient: bfloat16 [256, 2048, 768], P('expert', 'row'), may hold values from -6 to 6
- owners: int32 [8, 32], P('expert'), may hold values from 0 to 31, as said below
Outputs:
- new_momentum: bfloat16 [256, 2048, 768], P('expert', 'row')
- update: bfloat16 [256, 2048, 768], P('expert', 'row')
- owner_scale: float32 [8, 32], P('expert', 'row')
The draws below stay inside these ranges and needn't reach their ends.
Inputs may be any that keep to these rules, and one draw needn't show every extreme that they name: `owners`: in each row of the table every index appears exactly 1 times.
All inputs are finite; a program needn't handle non-finite values.
Results may differ from the reference program's by a relative error of at most 0.0085.
Values may be sent and summed in bfloat16 or wider, within the bound.
No kernel may reach another device: no remote copies, remote signals or barrier semaphores. Data moves between devices by JAX's collectives and lax.ppermute only.
A program may use at most 64 MiB of HBM per device.

```python
import math
import jax
import jax.numpy as jnp
from jax import lax

D = 2048
FF = 768
MAT_DEV = 1
ITERS = 2
MATS = 32
MATRICES = 256
N_EXPERT = 8
N_ROW = 32


def owner_row(single):
    pool = jnp.arange(MATS, dtype=jnp.int32) % N_ROW
    return jax.random.permutation(single, pool)


def draw_owners(key, part):
    keys = jax.random.split(jax.random.fold_in(key, 17), N_EXPERT)
    return jax.vmap(owner_row)(keys).astype(jnp.int32)


def level_of(stream_key, dims, shards, smallest, top_value):
    loudness, own = 1.0, jax.random.fold_in(stream_key, 6)
    for position, shards_of in shards:
        heights = jnp.exp(jax.random.uniform(jax.random.fold_in(own, position), (shards_of,), jnp.float32, smallest / len(shards), top_value / len(shards)))
        loudness = loudness * jnp.repeat(heights, dims[position] // shards_of).reshape([-1 if axis == position else 1 for axis in range(len(dims))])
    return loudness


def noise(own_key, extent, scale, bound, shards=(), kind=jnp.bfloat16):
    result = jax.random.normal(own_key, extent, jnp.float32) * scale
    if len(shards) > 0:
        result = level_of(own_key, extent, shards, -0.22, 0.18) * result
    return jnp.clip(result, min=-bound, max=bound).astype(kind)


def setup_inputs(seed: int = 0) -> dict:
    streams_of = jax.random.split(jax.random.key(seed), 4)
    momentum = noise(streams_of[0], (MATRICES, D, FF), 1.0, 6.0, ((0, 8), (1, 32)))
    gradient = noise(streams_of[1], (MATRICES, D, FF), 1.0, 6.0, ((0, 8), (1, 32)))
    owners = draw_owners(jax.random.fold_in(streams_of[3], 71), 0)
    return dict(momentum=momentum, gradient=gradient, owners=owners)


quintic_one = 3.4445
quintic_two = -4.775
quintic_three = 2.0315
momentum_beta = 0.95
clip_rms = 0.25

def newton_schulz(matrix):
    values = matrix.astype(jnp.float32)
    frobenius = jnp.sqrt(jnp.sum(values * values))
    iterate = (values / (frobenius + 1e-07)).astype(jnp.bfloat16)
    for step in range(ITERS):
        gram = jnp.dot(iterate.T, iterate, preferred_element_type=jnp.float32).astype(jnp.bfloat16)
        square = jnp.dot(gram, gram, preferred_element_type=jnp.float32)
        poly = (quintic_two * gram.astype(jnp.float32) + quintic_three * square).astype(jnp.bfloat16)
        product = jnp.dot(iterate, poly, preferred_element_type=jnp.float32)
        iterate = (quintic_one * iterate.astype(jnp.float32) + product).astype(jnp.bfloat16)
    update = (math.sqrt(D) * iterate.astype(jnp.float32)).astype(jnp.bfloat16)
    return (update, frobenius / math.sqrt(D * FF))

def reference(momentum, gradient, owners):
    grad_f32 = gradient.astype(jnp.float32)
    square_sum = jnp.sum(grad_f32 * grad_f32)
    entry_count = float(MATS * N_EXPERT * D * FF)
    factor = jnp.minimum(jnp.float32(1.0), clip_rms / jnp.sqrt(square_sum / entry_count + 1e-06))
    new_momentum = (momentum_beta * momentum.astype(jnp.float32) + factor * grad_f32).astype(jnp.bfloat16)
    updates, scales = lax.map(newton_schulz, new_momentum)
    scales = scales.reshape(N_EXPERT, MATS)
    positions = jnp.arange(MATS, dtype=jnp.int32)
    same = (owners[:, :, None] == owners[:, None, :]).astype(jnp.int32)
    earlier = (positions[None, :] < positions[:, None]).astype(jnp.int32)
    slot = lax.optimization_barrier(jnp.sum(same * earlier[None, :, :], axis=2)).astype(jnp.int32)
    code = owners * MAT_DEV + slot
    onehot = (code[:, :, None] == positions[None, None, :]).astype(scales.dtype)
    owner_scale = lax.optimization_barrier(jnp.sum(onehot * scales[:, :, None], axis=1))
    return (new_momentum, updates, owner_scale)
```

```python
import functools
import math

import jax
import jax.numpy as jnp
from jax import lax
from jax.experimental import pallas as pl
from jax.experimental.pallas import tpu as pltpu
from jax.sharding import Mesh
from jax.sharding import PartitionSpec as P

D = 2048
FF = 768
AXES = ("zh", "x", "y", "far", "near", "core")
SIZES = (2, 4, 4, 2, 2, 2)
EXPERT = ("zh", "x")
ROW = ("y", "far", "near", "core")
HALF = ("y", "near", "core")
HALF_SIZE = 16

quintic_one = 3.4445
quintic_two = -4.775
quintic_three = 2.0315
momentum_beta = 0.95
clip_rms = 0.25

B = 128
NB = FF // B
OFF = [(i, j) for i in range(NB) for j in range(i + 1, NB)]
PAIRS = [(i, i + 1) for i in range(0, NB, 2)]
TAIL = (len(OFF) + len(PAIRS)) * B
PACKED = TAIL + 16
f32 = jnp.float32
bf16 = jnp.bfloat16
VMEM = pl.BlockSpec(memory_space=pltpu.VMEM)


def square_kernel(g_ref, out_ref, acc):
    step = pl.program_id(0)
    values = g_ref[...].astype(f32).reshape(-1, 8, FF)
    part = jnp.sum(values * values, axis=0)

    @pl.when(step == 0)
    def _():
        acc[...] = part

    @pl.when(step > 0)
    def _():
        acc[...] += part

    @pl.when(step == pl.num_programs(0) - 1)
    def _():
        total = acc[:, 0:B]
        for j in range(1, NB):
            total = total + acc[:, j * B : (j + 1) * B]
        out_ref[...] = jnp.sum(total, axis=0, keepdims=True)


def local_squares(gradient):
    count = gradient.shape[0]
    return pl.pallas_call(
        square_kernel,
        grid=(4,),
        in_specs=[pl.BlockSpec((count // 4,) + gradient.shape[1:], lambda i: (i, 0, 0))],
        out_specs=pl.BlockSpec((1, B), lambda i: (0, 0)),
        out_shape=jax.ShapeDtypeStruct((1, B), f32),
        scratch_shapes=[pltpu.VMEM((8, FF), f32)],
        name="local_squares",
    )(gradient)


def rows_cols():
    return (
        lax.broadcasted_iota(jnp.int32, (B, B), 0),
        lax.broadcasted_iota(jnp.int32, (B, B), 1),
    )


def gram_kernel(m_ref, gram_ref, packed_ref):
    rows, cols = rows_cols()
    for i in range(3):
        lo = i * 256
        gram_ref[lo : lo + 256, lo:] = lax.dot_general(
            m_ref[:, lo : lo + 256], m_ref[:, lo:], (((0,), (0,)), ((), ())), preferred_element_type=f32
        )

    def block(i, j):
        return gram_ref[i * B : (i + 1) * B, j * B : (j + 1) * B]

    for k, (i, j) in enumerate(OFF):
        packed_ref[k * B : (k + 1) * B, :] = block(i, j).astype(bf16)
    diagonals = []
    squares = None
    for k, (i, j) in enumerate(PAIRS):
        first, second = block(i, i), block(j, j)
        lo = (len(OFF) + k) * B
        packed_ref[lo : lo + B, :] = jnp.where(rows <= cols, first, second).astype(bf16)
        diagonal = jnp.sum(jnp.where(rows == cols, second, 0.0), axis=0, keepdims=True)
        both = jnp.sum(jnp.where(rows == cols, first, 0.0), axis=0, keepdims=True) + diagonal
        diagonals.append(diagonal)
        squares = both if squares is None else squares + both
    high = squares.astype(bf16).astype(f32)
    middle = (squares - high).astype(bf16).astype(f32)
    low = squares - high - middle
    tail_rows = diagonals + [high, middle, low]
    place = lax.broadcasted_iota(jnp.int32, (16, B), 0)
    tail = jnp.zeros((16, B), f32)
    for r, row in enumerate(tail_rows):
        tail = jnp.where(place == r, jnp.broadcast_to(row, (16, B)), tail)
    packed_ref[TAIL:, :] = tail.astype(bf16)


def partial_gram(part):
    return pl.pallas_call(
        gram_kernel,
        in_specs=[VMEM],
        out_specs=[VMEM, VMEM],
        out_shape=[
            jax.ShapeDtypeStruct((FF, FF), f32),
            jax.ShapeDtypeStruct((PACKED, B), bf16),
        ],
        name="partial_gram",
        cost_estimate=pl.CostEstimate(flops=2 * part.shape[0] * FF * FF, bytes_accessed=5_000_000, transcendentals=0),
    )(part)


def update_kernel(m_ref, own_ref, packed_ref, u_ref, fro_ref, gf, gb, pb, g1b, p1b, qb):
    rows, cols = rows_cols()
    tail = packed_ref[TAIL:, :].astype(f32)
    squares = tail[3:4, :] + tail[4:5, :] + tail[5:6, :]
    for i in range(NB):
        own = own_ref[i * B : (i + 1) * B, i * B : (i + 1) * B]
        squares = squares + jnp.sum(jnp.where(rows == cols, own, 0.0), axis=0, keepdims=True)
    frobenius = jnp.sqrt(jnp.sum(squares, axis=1, keepdims=True))
    fro_ref[...] = jnp.broadcast_to(frobenius, (1, B))
    scale = 1.0 / (frobenius + 1e-07)
    scale2 = scale * scale

    def put(i, j, value):
        gf[i * B : (i + 1) * B, j * B : (j + 1) * B] = value
        gb[i * B : (i + 1) * B, j * B : (j + 1) * B] = value.astype(bf16)

    def own_block(i, j):
        return own_ref[i * B : (i + 1) * B, j * B : (j + 1) * B]

    for k, (i, j) in enumerate(OFF):
        value = (own_block(i, j) + packed_ref[k * B : (k + 1) * B, :].astype(f32)) * scale2
        put(i, j, value)
        put(j, i, value.T)
    for k, (i, j) in enumerate(PAIRS):
        lo = (len(OFF) + k) * B
        merged = packed_ref[lo : lo + B, :].astype(f32)
        turned = merged.T
        first = jnp.where(rows <= cols, merged, turned)
        second = jnp.where(rows > cols, merged, turned)
        second = jnp.where(rows == cols, jnp.broadcast_to(tail[k : k + 1, :], (B, B)), second)
        put(i, i, (own_block(i, i) + first) * scale2)
        put(j, j, (own_block(j, j) + second) * scale2)

    a, b, c = quintic_one, quintic_two, quintic_three
    strips = [slice(i * 256, (i + 1) * 256) for i in range(3)]
    for s in strips:
        square = jnp.dot(gb[s, :], gb[...], preferred_element_type=f32)
        pb[s, :] = (b * gf[s, :] + c * square).astype(bf16)
    for s in strips:
        gp = jnp.dot(gb[s, :], pb[...], preferred_element_type=f32)
        pgp = jnp.dot(gp.astype(bf16), pb[...], preferred_element_type=f32)
        g1b[s, :] = (a * a * gf[s, :] + 2.0 * a * gp + pgp).astype(bf16)
    for s in strips:
        square = jnp.dot(g1b[s, :], g1b[...], preferred_element_type=f32)
        p1b[s, :] = (b * g1b[s, :].astype(f32) + c * square).astype(bf16)
    for s in strips:
        product = jnp.dot(pb[s, :], p1b[...], preferred_element_type=f32)
        qb[s, :] = (a * (pb[s, :].astype(f32) + p1b[s, :].astype(f32)) + product).astype(bf16)
    last = scale * math.sqrt(D)
    for r in range(m_ref.shape[0] // 256):
        s = slice(r * 256, (r + 1) * 256)
        product = jnp.dot(m_ref[s, :], qb[...], preferred_element_type=f32)
        u_ref[s, :] = ((a * a * m_ref[s, :].astype(f32) + product) * last).astype(bf16)


def orthogonal_rows(part, own, packed):
    square = pltpu.VMEM((FF, FF), bf16)
    return pl.pallas_call(
        update_kernel,
        in_specs=[VMEM, VMEM, VMEM],
        out_specs=[VMEM, VMEM],
        out_shape=[
            jax.ShapeDtypeStruct(part.shape, bf16),
            jax.ShapeDtypeStruct((1, B), f32),
        ],
        scratch_shapes=[pltpu.VMEM((FF, FF), f32), square, square, square, square, square],
        name="orthogonal_rows",
        cost_estimate=pl.CostEstimate(
            flops=10 * FF**3 + 2 * part.shape[0] * FF * FF, bytes_accessed=6_000_000, transcendentals=0
        ),
    )(part, own, packed)


def swap(x, axis):
    return lax.ppermute(x, axis, [(0, 1), (1, 0)])


def local(momentum, gradient, owners):
    matrix_count = momentum.shape[0]
    row_count = momentum.shape[1]
    half = matrix_count // 2

    squares = local_squares(gradient)
    everyone = lax.axis_size(AXES)
    gathered = lax.all_to_all(
        jnp.broadcast_to(squares[None], (everyone, 1, B)), AXES, 0, 0, tiled=True
    )
    entry_count = float(everyone * gradient.size)
    factor = jnp.minimum(f32(1.0), clip_rms / jnp.sqrt(jnp.sum(gathered) / entry_count + 1e-06))

    def step(m, g):
        return (momentum_beta * m.astype(f32) + factor * g.astype(f32)).astype(bf16)

    parts = [step(momentum[i * half : (i + 1) * half], gradient[i * half : (i + 1) * half]) for i in range(2)]
    new_momentum = step(momentum, gradient)

    def gather(part):
        rows = lax.all_to_all(part, HALF, 0, 0, tiled=True)
        return rows.reshape(HALF_SIZE * row_count, FF)

    def scatter(update):
        return lax.all_to_all(update.reshape(HALF_SIZE, row_count, FF), HALF, 0, 0, tiled=True)

    rows = [gather(part) for part in parts]
    grams = [partial_gram(r) for r in rows]
    others = [swap(packed, "far") for _, packed in grams]
    others[0], sent = lax.optimization_barrier((others[0], grams[1][1]))
    first, first_norm = orthogonal_rows(rows[0], grams[0][0], others[0])
    second, second_norm = orthogonal_rows(rows[1], grams[1][0], others[1])
    froes = [first_norm, second_norm]
    updates = [scatter(first), scatter(second)]

    lanes = lax.broadcasted_iota(jnp.int32, (HALF_SIZE, B), 1)
    place = lax.broadcasted_iota(jnp.int32, (HALF_SIZE, B), 0)
    both = jnp.where(lanes == 0, froes[0], jnp.where(lanes == 1, froes[1], 0.0))
    norms = jnp.where(place == lax.axis_index(HALF), both, 0.0)
    norms = norms + swap(norms, "core")
    norms = norms + swap(norms, "near")
    norms = norms + lax.ppermute(norms, "y", [(i, i ^ 1) for i in range(4)])
    norms = norms + lax.ppermute(norms, "y", [(i, i ^ 2) for i in range(4)])
    norms = norms[:, :2].T.reshape(matrix_count)
    mine = owners[0] == lax.axis_index(ROW)
    scale = jnp.sum(jnp.where(mine, norms, 0.0)) / math.sqrt(D * FF)
    return (new_momentum, jnp.concatenate(updates, axis=0), scale.reshape(1, 1))


def solution(mesh):
    torus = Mesh(mesh.devices.reshape(SIZES), AXES)
    in_specs = (P(EXPERT, ROW, None), P(EXPERT, ROW, None), P(EXPERT, None))
    out_specs = (P(EXPERT, ROW, None), P(EXPERT, ROW, None), P(EXPERT, ROW))
    return jax.shard_map(local, mesh=torus, in_specs=in_specs, out_specs=out_specs, check_vma=False)
```

```python
import functools
import math

import jax
import jax.numpy as jnp
from jax import lax
from jax.experimental import pallas as pl
from jax.experimental.pallas import tpu as pltpu
from jax.sharding import Mesh
from jax.sharding import PartitionSpec as P

D = 2048
FF = 768
AXES = ("zh", "x", "y", "far", "near", "core")
SIZES = (2, 4, 4, 2, 2, 2)
EXPERT = ("zh", "x")
ROW = ("y", "far", "near", "core")
HALF = ("y", "near", "core")
HALF_SIZE = 16

quintic_one = 3.4445
quintic_two = -4.775
quintic_three = 2.0315
momentum_beta = 0.95
clip_rms = 0.25

B = 128
NB = FF // B
OFF = [(i, j) for i in range(NB) for j in range(i + 1, NB)]
PAIRS = [(i, i + 1) for i in range(0, NB, 2)]
TAIL = (len(OFF) + len(PAIRS)) * B
PACKED = TAIL + 16
UPDATE_STRIPS = 4
f32 = jnp.float32
bf16 = jnp.bfloat16
VMEM = pl.BlockSpec(memory_space=pltpu.VMEM)


def square_kernel(g_ref, out_ref, acc):
    step = pl.program_id(0)

    @pl.when(step == 0)
    def _():
        acc[...] = jnp.zeros_like(acc)

    def body(k, total):
        values = g_ref[k].astype(f32)
        return total + jnp.sum((values * values).reshape(-1, 8, FF), axis=0)

    acc[...] = lax.fori_loop(0, g_ref.shape[0], body, acc[...])

    @pl.when(step == pl.num_programs(0) - 1)
    def _():
        total = acc[:, 0:B]
        for j in range(1, NB):
            total = total + acc[:, j * B : (j + 1) * B]
        total = jnp.sum(total, axis=0, keepdims=True)
        out_ref[...] = jnp.broadcast_to(total[None], out_ref.shape)


def local_squares(gradient, copies):
    count = gradient.shape[0]
    return pl.pallas_call(
        square_kernel,
        grid=(4,),
        in_specs=[pl.BlockSpec((count // 4,) + gradient.shape[1:], lambda i: (i, 0, 0))],
        out_specs=pl.BlockSpec((copies, 1, B), lambda i: (0, 0, 0)),
        out_shape=jax.ShapeDtypeStruct((copies, 1, B), f32),
        scratch_shapes=[pltpu.VMEM((8, FF), f32)],
        compiler_params=pltpu.CompilerParams(vmem_limit_bytes=16 << 20),
        name="local_squares",
    )(gradient)


def clip_factor(squares_ref, entry_count):
    total = jnp.sum(squares_ref[:, 0, :], axis=0, keepdims=True)
    total = jnp.sum(total, axis=1, keepdims=True)
    return jnp.minimum(f32(1.0), clip_rms / jnp.sqrt(total / entry_count + 1e-06))


STEP = 4


def step_kernel(entry_count, squares_ref, m_ref, g_ref, out_ref, new_ref, sems):
    factor = clip_factor(squares_ref, entry_count)
    copies = []
    for i in range(new_ref.shape[0] // STEP):
        for k in range(i * STEP, (i + 1) * STEP):
            new = momentum_beta * m_ref[k].astype(f32) + factor * g_ref[k].astype(f32)
            new_ref[k] = new.astype(bf16)
        part = pl.ds(i * STEP, STEP)
        copies.append(pltpu.make_async_copy(new_ref.at[part], out_ref.at[part], sems.at[i]))
        copies[-1].start()
    for copy in copies:
        copy.wait()


def first_step(squares, momentum, gradient, entry_count):
    shape = (momentum.shape[0] // 2,) + momentum.shape[1:]
    return pl.pallas_call(
        functools.partial(step_kernel, entry_count),
        in_specs=[VMEM, VMEM, VMEM],
        out_specs=pl.BlockSpec(memory_space=pltpu.HBM),
        out_shape=pltpu.HBM(shape, bf16),
        scratch_shapes=[pltpu.VMEM(shape, bf16), pltpu.SemaphoreType.DMA((shape[0] // STEP,))],
        compiler_params=pltpu.CompilerParams(vmem_limit_bytes=16 << 20),
        name="first_step",
    )(squares, momentum, gradient)


def whole_step_kernel(entry_count, squares_ref, m_ref, g_ref, new_ref, second_ref, sums_ref):
    step = pl.program_id(0)
    factor = clip_factor(squares_ref, entry_count)
    lanes = lax.broadcasted_iota(jnp.int32, (1, B), 1)

    @pl.when(step == 0)
    def _():
        sums_ref[...] = jnp.zeros_like(sums_ref)

    sums = sums_ref[...]
    for k in range(m_ref.shape[0]):
        new = momentum_beta * m_ref[k].astype(f32) + factor * g_ref[k].astype(f32)
        new = new.astype(bf16)
        new_ref[k] = new
        second_ref[k] = new
        values = new.astype(f32)
        part = jnp.sum((values * values).reshape(-1, 8, FF), axis=0)
        part = jnp.sum(jnp.sum(part, axis=0, keepdims=True), axis=1, keepdims=True)
        sums = sums + jnp.where(lanes == step * STEP + k, part, 0.0)
    sums_ref[...] = sums


def whole_step(squares, momentum, gradient, entry_count):
    count = momentum.shape[0]
    first = count // 2 // STEP
    block = pl.BlockSpec((STEP,) + momentum.shape[1:], lambda i: (i, 0, 0))
    second = pl.BlockSpec((STEP,) + momentum.shape[1:], lambda i: (jnp.maximum(i - first, 0), 0, 0))
    return pl.pallas_call(
        functools.partial(whole_step_kernel, entry_count),
        grid=(count // STEP,),
        in_specs=[pl.BlockSpec(squares.shape, lambda i: (0, 0, 0)), block, block],
        out_specs=[block, second, pl.BlockSpec((1, B), lambda i: (0, 0))],
        out_shape=[
            jax.ShapeDtypeStruct(momentum.shape, bf16),
            pltpu.HBM((count // 2,) + momentum.shape[1:], bf16),
            jax.ShapeDtypeStruct((1, B), f32),
        ],
        compiler_params=pltpu.CompilerParams(vmem_limit_bytes=16 << 20),
        name="whole_step",
    )(squares, momentum, gradient)


def place_kernel(offset, part_ref, *refs):
    out_ref, sems = refs[-2:]
    copies = []
    for i in range(part_ref.shape[0] // STEP):
        source = part_ref.at[pl.ds(i * STEP, STEP)]
        target = out_ref.at[pl.ds(offset + i * STEP, STEP)]
        copies.append(pltpu.make_async_copy(source, target, sems.at[i]))
        copies[-1].start()
    for copy in copies:
        copy.wait()


def place(part, offset, count, into=None):
    operands = [part] if into is None else [part, into]
    return pl.pallas_call(
        functools.partial(place_kernel, offset),
        in_specs=[pl.BlockSpec(memory_space=pl.ANY)] * len(operands),
        out_specs=pl.BlockSpec(memory_space=pltpu.HBM),
        out_shape=pltpu.HBM((count,) + part.shape[1:], bf16),
        scratch_shapes=[pltpu.SemaphoreType.DMA((part.shape[0] // STEP,))],
        input_output_aliases={} if into is None else {1: 0},
        compiler_params=pltpu.CompilerParams(vmem_limit_bytes=16 << 20),
        name="place",
    )(*operands)


def rows_cols():
    return (
        lax.broadcasted_iota(jnp.int32, (B, B), 0),
        lax.broadcasted_iota(jnp.int32, (B, B), 1),
    )


def three_parts(value):
    high = value.astype(bf16).astype(f32)
    middle = (value - high).astype(bf16).astype(f32)
    return [high, middle, value - high - middle]


def gram_kernel(m_ref, sums_ref, packed_ref, gram_ref):
    rows, cols = rows_cols()
    for i in range(3):
        lo = i * 256
        gram_ref[lo : lo + 256, lo:] = lax.dot_general(
            m_ref[:, lo : lo + 256], m_ref[:, lo:], (((0,), (0,)), ((), ())), preferred_element_type=f32
        )

    def block(i, j):
        return gram_ref[i * B : (i + 1) * B, j * B : (j + 1) * B]

    for k, (i, j) in enumerate(OFF):
        packed_ref[k * B : (k + 1) * B, :] = block(i, j).astype(bf16)
    diagonals = []
    squares = None
    for k, (i, j) in enumerate(PAIRS):
        first, second = block(i, i), block(j, j)
        lo = (len(OFF) + k) * B
        packed_ref[lo : lo + B, :] = jnp.where(rows <= cols, first, second).astype(bf16)
        diagonal = jnp.sum(jnp.where(rows == cols, second, 0.0), axis=0, keepdims=True)
        both = jnp.sum(jnp.where(rows == cols, first, 0.0), axis=0, keepdims=True) + diagonal
        diagonals.append(diagonal)
        squares = both if squares is None else squares + both
    tail_rows = diagonals + three_parts(squares) + three_parts(sums_ref[...])
    place = lax.broadcasted_iota(jnp.int32, (16, B), 0)
    tail = jnp.zeros((16, B), f32)
    for r, row in enumerate(tail_rows):
        tail = jnp.where(place == r, jnp.broadcast_to(row, (16, B)), tail)
    packed_ref[TAIL:, :] = tail.astype(bf16)


def partial_gram(part, sums):
    return pl.pallas_call(
        gram_kernel,
        in_specs=[VMEM, VMEM],
        out_specs=VMEM,
        out_shape=jax.ShapeDtypeStruct((PACKED, B), bf16),
        scratch_shapes=[pltpu.VMEM((FF, FF), f32)],
        compiler_params=pltpu.CompilerParams(vmem_limit_bytes=24 << 20),
        name="partial_gram",
        cost_estimate=pl.CostEstimate(flops=2 * part.shape[0] * FF * FF, bytes_accessed=2_000_000, transcendentals=0),
    )(part, sums)


def update_kernel(m_ref, own_ref, other_ref, out_ref, gf, gb, pb, g1b, p1b, qb, u_ref, sems):
    rows, cols = rows_cols()

    def summed(lo, size):
        return own_ref[lo : lo + size, :].astype(f32) + other_ref[lo : lo + size, :].astype(f32)

    tail = summed(TAIL, 16)
    squares = jnp.sum(tail[3:6, :], axis=0, keepdims=True)
    frobenius = jnp.sqrt(jnp.sum(squares, axis=1, keepdims=True))
    scale = 1.0 / (frobenius + 1e-07)
    scale2 = scale * scale

    def put(i, j, value):
        gf[i * B : (i + 1) * B, j * B : (j + 1) * B] = value
        gb[i * B : (i + 1) * B, j * B : (j + 1) * B] = value.astype(bf16)

    for k, (i, j) in enumerate(OFF):
        value = summed(k * B, B) * scale2
        put(i, j, value)
        put(j, i, value.T)
    for k, (i, j) in enumerate(PAIRS):
        merged = summed((len(OFF) + k) * B, B) * scale2
        turned = merged.T
        put(i, i, jnp.where(rows <= cols, merged, turned))
        second = jnp.where(rows > cols, merged, turned)
        put(j, j, jnp.where(rows == cols, jnp.broadcast_to(tail[k : k + 1, :] * scale2, (B, B)), second))

    a, b, c = quintic_one, quintic_two, quintic_three
    strips = [slice(i * 256, (i + 1) * 256) for i in range(3)]
    for s in strips:
        square = jnp.dot(gb[s, :], gb[...], preferred_element_type=f32)
        pb[s, :] = (b * gf[s, :] + c * square).astype(bf16)
    for s in strips:
        gp = jnp.dot(gb[s, :], pb[...], preferred_element_type=f32)
        pgp = jnp.dot(gp.astype(bf16), pb[...], preferred_element_type=f32)
        g1b[s, :] = (a * a * gf[s, :] + 2.0 * a * gp + pgp).astype(bf16)
    for s in strips:
        square = jnp.dot(g1b[s, :], g1b[...], preferred_element_type=f32)
        p1b[s, :] = (b * g1b[s, :].astype(f32) + c * square).astype(bf16)
    for s in strips:
        product = jnp.dot(pb[s, :], p1b[...], preferred_element_type=f32)
        qb[s, :] = (a * (pb[s, :].astype(f32) + p1b[s, :].astype(f32)) + product).astype(bf16)
    last = scale * math.sqrt(D)
    copies = []
    for r in range(UPDATE_STRIPS):
        s = pl.ds(r * 256, 256)
        product = jnp.dot(m_ref[s, :], qb[...], preferred_element_type=f32)
        u_ref[s, :] = ((a * a * m_ref[s, :].astype(f32) + product) * last).astype(bf16)
        copies.append(pltpu.make_async_copy(u_ref.at[s, :], out_ref.at[s, :], sems.at[r]))
        copies[-1].start()
    for copy in copies:
        copy.wait()


def orthogonal_rows(part, own, other):
    square = pltpu.VMEM((FF, FF), bf16)
    return pl.pallas_call(
        update_kernel,
        in_specs=[VMEM, VMEM, VMEM],
        out_specs=pl.BlockSpec(memory_space=pltpu.HBM),
        out_shape=pltpu.HBM(part.shape, bf16),
        scratch_shapes=[
            pltpu.VMEM((FF, FF), f32),
            square,
            square,
            square,
            square,
            square,
            pltpu.VMEM(part.shape, bf16),
            pltpu.SemaphoreType.DMA((UPDATE_STRIPS,)),
        ],
        compiler_params=pltpu.CompilerParams(vmem_limit_bytes=32 << 20),
        name="orthogonal_rows",
        cost_estimate=pl.CostEstimate(flops=60_000_000_000, bytes_accessed=6_000_000, transcendentals=0),
    )(part, own, other)


def swap(x, axis):
    return lax.ppermute(x, axis, [(0, 1), (1, 0)])


def local(momentum, gradient, owners):
    matrix_count = momentum.shape[0]
    row_count = momentum.shape[1]
    half = matrix_count // 2

    everyone = lax.axis_size(AXES)
    entry_count = float(everyone * gradient.size)
    squares = lax.all_to_all(local_squares(gradient, everyone), AXES, 0, 0, tiled=True)

    def gather(part):
        rows = lax.all_to_all(part, HALF, 0, 0, tiled=True)
        return rows.reshape(HALF_SIZE * row_count, FF)

    def scatter(update):
        return lax.all_to_all(update.reshape(HALF_SIZE, row_count, FF), HALF, 0, 0, tiled=True)

    first = gather(first_step(squares, momentum, gradient, entry_count))
    new_momentum, second, sums = whole_step(squares, momentum, gradient, entry_count)
    sums = sums + swap(sums, "core")
    sums = sums + swap(sums, "near")
    first, sums = lax.optimization_barrier((first, sums))
    own_first = partial_gram(first, sums)
    second, own_first = lax.optimization_barrier((second, own_first))
    other_first = swap(own_first, "far")
    rows = gather(second)
    both = own_first[TAIL + 6 : TAIL + 9].astype(f32) + other_first[TAIL + 6 : TAIL + 9].astype(f32)
    sums = jnp.sum(both, axis=0, keepdims=True)
    around = [lax.ppermute(sums, "y", [(i, (i + k) % 4) for i in range(4)]) for k in range(1, 4)]
    first = orthogonal_rows(first, own_first, other_first)
    sums = functools.reduce(jnp.add, around, sums)
    rows, first, sums = lax.optimization_barrier((rows, first, sums))
    own_second = partial_gram(rows, sums)
    other_second = swap(own_second, "far")
    first, own_second = lax.optimization_barrier((first, own_second))
    first = scatter(first)
    second = scatter(orthogonal_rows(rows, own_second, other_second))
    updates = place(first, 0, matrix_count)
    updates = place(second, half, matrix_count, updates)

    mine = owners[0] == lax.axis_index(ROW)
    norm = jnp.sqrt(jnp.sum(jnp.where(mine, sums[0, :matrix_count], 0.0)))
    return (new_momentum, updates, (norm / math.sqrt(D * FF)).reshape(1, 1))


def solution(mesh):
    torus = Mesh(mesh.devices.reshape(SIZES), AXES)
    in_specs = (P(EXPERT, ROW, None), P(EXPERT, ROW, None), P(EXPERT, None))
    out_specs = (P(EXPERT, ROW, None), P(EXPERT, ROW, None), P(EXPERT, ROW))
    return jax.shard_map(local, mesh=torus, in_specs=in_specs, out_specs=out_specs, check_vma=False)
```

```python
import functools
import math

import jax
import jax.numpy as jnp
from jax import lax
from jax.experimental import pallas as pl
from jax.experimental.pallas import tpu as pltpu
from jax.sharding import Mesh
from jax.sharding import PartitionSpec as P

D = 2048
FF = 768
AXES = ("zh", "x", "y", "far", "near", "core")
SIZES = (2, 4, 4, 2, 2, 2)
EXPERT = ("zh", "x")
ROW = ("y", "far", "near", "core")
HALF = ("y", "near", "core")
HALF_SIZE = 16

quintic_one = 3.4445
quintic_two = -4.775
quintic_three = 2.0315
momentum_beta = 0.95
clip_rms = 0.25

B = 128
NB = FF // B
OFF = [(i, j) for i in range(NB) for j in range(i + 1, NB)]
PAIRS = [(i, i + 1) for i in range(0, NB, 2)]
TAIL = (len(OFF) + len(PAIRS)) * B
PACKED = TAIL + 16
UPDATE_STRIPS = 4
f32 = jnp.float32
bf16 = jnp.bfloat16
VMEM = pl.BlockSpec(memory_space=pltpu.VMEM)


def square_kernel(g_ref, out_ref, acc):
    step = pl.program_id(0)

    @pl.when(step == 0)
    def _():
        acc[...] = jnp.zeros_like(acc)

    def body(k, total):
        values = g_ref[k].astype(f32)
        return total + jnp.sum((values * values).reshape(-1, 8, FF), axis=0)

    acc[...] = lax.fori_loop(0, g_ref.shape[0], body, acc[...])

    @pl.when(step == pl.num_programs(0) - 1)
    def _():
        total = acc[:, 0:B]
        for j in range(1, NB):
            total = total + acc[:, j * B : (j + 1) * B]
        total = jnp.sum(total, axis=0, keepdims=True)
        out_ref[...] = jnp.broadcast_to(total[None], out_ref.shape)


def local_squares(gradient, copies):
    count = gradient.shape[0]
    return pl.pallas_call(
        square_kernel,
        grid=(4,),
        in_specs=[pl.BlockSpec((count // 4,) + gradient.shape[1:], lambda i: (i, 0, 0))],
        out_specs=pl.BlockSpec((copies, 1, B), lambda i: (0, 0, 0)),
        out_shape=jax.ShapeDtypeStruct((copies, 1, B), f32),
        scratch_shapes=[pltpu.VMEM((8, FF), f32)],
        compiler_params=pltpu.CompilerParams(vmem_limit_bytes=16 << 20),
        name="local_squares",
    )(gradient)


def clip_factor(squares_ref, entry_count):
    total = jnp.sum(squares_ref[:, 0, :], axis=0, keepdims=True)
    total = jnp.sum(total, axis=1, keepdims=True)
    return jnp.minimum(f32(1.0), clip_rms / jnp.sqrt(total / entry_count + 1e-06))


STEP = 4


def step_kernel(entry_count, squares_ref, m_ref, g_ref, out_ref, new_ref, sems):
    factor = clip_factor(squares_ref, entry_count)
    copies = []
    for i in range(new_ref.shape[0] // STEP):
        for k in range(i * STEP, (i + 1) * STEP):
            new = momentum_beta * m_ref[k].astype(f32) + factor * g_ref[k].astype(f32)
            new_ref[k] = new.astype(bf16)
        part = pl.ds(i * STEP, STEP)
        copies.append(pltpu.make_async_copy(new_ref.at[part], out_ref.at[part], sems.at[i]))
        copies[-1].start()
    for copy in copies:
        copy.wait()


def first_step(squares, momentum, gradient, entry_count):
    shape = (momentum.shape[0] // 2,) + momentum.shape[1:]
    return pl.pallas_call(
        functools.partial(step_kernel, entry_count),
        in_specs=[VMEM, VMEM, VMEM],
        out_specs=pl.BlockSpec(memory_space=pltpu.HBM),
        out_shape=pltpu.HBM(shape, bf16),
        scratch_shapes=[pltpu.VMEM(shape, bf16), pltpu.SemaphoreType.DMA((shape[0] // STEP,))],
        compiler_params=pltpu.CompilerParams(vmem_limit_bytes=16 << 20),
        name="first_step",
    )(squares, momentum, gradient)


def whole_step_kernel(entry_count, squares_ref, m_ref, g_ref, new_ref, second_ref, sums_ref):
    step = pl.program_id(0)
    factor = clip_factor(squares_ref, entry_count)
    lanes = lax.broadcasted_iota(jnp.int32, (1, B), 1)

    @pl.when(step == 0)
    def _():
        sums_ref[...] = jnp.zeros_like(sums_ref)

    sums = sums_ref[...]
    for k in range(m_ref.shape[0]):
        new = momentum_beta * m_ref[k].astype(f32) + factor * g_ref[k].astype(f32)
        new = new.astype(bf16)
        new_ref[k] = new
        second_ref[k] = new
        values = new.astype(f32)
        part = jnp.sum((values * values).reshape(-1, 8, FF), axis=0)
        part = jnp.sum(jnp.sum(part, axis=0, keepdims=True), axis=1, keepdims=True)
        sums = sums + jnp.where(lanes == step * STEP + k, part, 0.0)
    sums_ref[...] = sums


def whole_step(squares, momentum, gradient, entry_count):
    count = momentum.shape[0]
    first = count // 2 // STEP
    block = pl.BlockSpec((STEP,) + momentum.shape[1:], lambda i: (i, 0, 0))
    second = pl.BlockSpec((STEP,) + momentum.shape[1:], lambda i: (jnp.maximum(i - first, 0), 0, 0))
    return pl.pallas_call(
        functools.partial(whole_step_kernel, entry_count),
        grid=(count // STEP,),
        in_specs=[pl.BlockSpec(squares.shape, lambda i: (0, 0, 0)), block, block],
        out_specs=[block, second, pl.BlockSpec((1, B), lambda i: (0, 0))],
        out_shape=[
            jax.ShapeDtypeStruct(momentum.shape, bf16),
            pltpu.HBM((count // 2,) + momentum.shape[1:], bf16),
            jax.ShapeDtypeStruct((1, B), f32),
        ],
        compiler_params=pltpu.CompilerParams(vmem_limit_bytes=16 << 20),
        name="whole_step",
    )(squares, momentum, gradient)


def place_kernel(offset, part_ref, *refs):
    out_ref, sems = refs[-2:]
    copies = []
    for i in range(part_ref.shape[0] // STEP):
        source = part_ref.at[pl.ds(i * STEP, STEP)]
        target = out_ref.at[pl.ds(offset + i * STEP, STEP)]
        copies.append(pltpu.make_async_copy(source, target, sems.at[i]))
        copies[-1].start()
    for copy in copies:
        copy.wait()


def place(part, offset, count, into=None):
    operands = [part] if into is None else [part, into]
    return pl.pallas_call(
        functools.partial(place_kernel, offset),
        in_specs=[pl.BlockSpec(memory_space=pl.ANY)] * len(operands),
        out_specs=pl.BlockSpec(memory_space=pltpu.HBM),
        out_shape=pltpu.HBM((count,) + part.shape[1:], bf16),
        scratch_shapes=[pltpu.SemaphoreType.DMA((part.shape[0] // STEP,))],
        input_output_aliases={} if into is None else {1: 0},
        compiler_params=pltpu.CompilerParams(vmem_limit_bytes=16 << 20),
        name="place",
    )(*operands)


def rows_cols():
    return (
        lax.broadcasted_iota(jnp.int32, (B, B), 0),
        lax.broadcasted_iota(jnp.int32, (B, B), 1),
    )


def three_parts(value):
    high = value.astype(bf16).astype(f32)
    middle = (value - high).astype(bf16).astype(f32)
    return [high, middle, value - high - middle]


def gram_kernel(m_ref, sums_ref, packed_ref, gram_ref):
    rows, cols = rows_cols()
    for i in range(3):
        lo = i * 256
        gram_ref[lo : lo + 256, lo:] = lax.dot_general(
            m_ref[:, lo : lo + 256], m_ref[:, lo:], (((0,), (0,)), ((), ())), preferred_element_type=f32
        )

    def block(i, j):
        return gram_ref[i * B : (i + 1) * B, j * B : (j + 1) * B]

    for k, (i, j) in enumerate(OFF):
        packed_ref[k * B : (k + 1) * B, :] = block(i, j).astype(bf16)
    diagonals = []
    squares = None
    for k, (i, j) in enumerate(PAIRS):
        first, second = block(i, i), block(j, j)
        lo = (len(OFF) + k) * B
        packed_ref[lo : lo + B, :] = jnp.where(rows <= cols, first, second).astype(bf16)
        diagonal = jnp.sum(jnp.where(rows == cols, second, 0.0), axis=0, keepdims=True)
        both = jnp.sum(jnp.where(rows == cols, first, 0.0), axis=0, keepdims=True) + diagonal
        diagonals.append(diagonal)
        squares = both if squares is None else squares + both
    tail_rows = diagonals + three_parts(squares) + three_parts(sums_ref[...])
    place = lax.broadcasted_iota(jnp.int32, (16, B), 0)
    tail = jnp.zeros((16, B), f32)
    for r, row in enumerate(tail_rows):
        tail = jnp.where(place == r, jnp.broadcast_to(row, (16, B)), tail)
    packed_ref[TAIL:, :] = tail.astype(bf16)


def partial_gram(part, sums):
    return pl.pallas_call(
        gram_kernel,
        in_specs=[VMEM, VMEM],
        out_specs=VMEM,
        out_shape=jax.ShapeDtypeStruct((PACKED, B), bf16),
        scratch_shapes=[pltpu.VMEM((FF, FF), f32)],
        compiler_params=pltpu.CompilerParams(vmem_limit_bytes=24 << 20),
        name="partial_gram",
        cost_estimate=pl.CostEstimate(flops=2 * part.shape[0] * FF * FF, bytes_accessed=2_000_000, transcendentals=0),
    )(part, sums)


def update_kernel(m_ref, own_ref, other_ref, out_ref, gf, gb, pb, g1b, p1b, qb, u_ref, sems):
    rows, cols = rows_cols()

    def summed(lo, size):
        return own_ref[lo : lo + size, :].astype(f32) + other_ref[lo : lo + size, :].astype(f32)

    tail = summed(TAIL, 16)
    squares = jnp.sum(tail[3:6, :], axis=0, keepdims=True)
    frobenius = jnp.sqrt(jnp.sum(squares, axis=1, keepdims=True))
    scale = 1.0 / (frobenius + 1e-07)
    scale2 = scale * scale

    def put(i, j, value):
        gf[i * B : (i + 1) * B, j * B : (j + 1) * B] = value
        gb[i * B : (i + 1) * B, j * B : (j + 1) * B] = value.astype(bf16)

    for k, (i, j) in enumerate(OFF):
        value = summed(k * B, B) * scale2
        put(i, j, value)
        put(j, i, value.T)
    for k, (i, j) in enumerate(PAIRS):
        merged = summed((len(OFF) + k) * B, B) * scale2
        turned = merged.T
        put(i, i, jnp.where(rows <= cols, merged, turned))
        second = jnp.where(rows > cols, merged, turned)
        put(j, j, jnp.where(rows == cols, jnp.broadcast_to(tail[k : k + 1, :] * scale2, (B, B)), second))

    a, b, c = quintic_one, quintic_two, quintic_three
    strips = [slice(i * 256, (i + 1) * 256) for i in range(3)]
    for s in strips:
        square = jnp.dot(gb[s, :], gb[...], preferred_element_type=f32)
        pb[s, :] = (b * gf[s, :] + c * square).astype(bf16)
    for s in strips:
        gp = jnp.dot(gb[s, :], pb[...], preferred_element_type=f32)
        pgp = jnp.dot(gp.astype(bf16), pb[...], preferred_element_type=f32)
        g1b[s, :] = (a * a * gf[s, :] + 2.0 * a * gp + pgp).astype(bf16)
    for s in strips:
        square = jnp.dot(g1b[s, :], g1b[...], preferred_element_type=f32)
        p1b[s, :] = (b * g1b[s, :].astype(f32) + c * square).astype(bf16)
    for s in strips:
        product = jnp.dot(pb[s, :], p1b[...], preferred_element_type=f32)
        qb[s, :] = (a * (pb[s, :].astype(f32) + p1b[s, :].astype(f32)) + product).astype(bf16)
    last = scale * math.sqrt(D)
    copies = []
    for r in range(UPDATE_STRIPS):
        s = pl.ds(r * 256, 256)
        product = jnp.dot(m_ref[s, :], qb[...], preferred_element_type=f32)
        u_ref[s, :] = ((a * a * m_ref[s, :].astype(f32) + product) * last).astype(bf16)
        copies.append(pltpu.make_async_copy(u_ref.at[s, :], out_ref.at[s, :], sems.at[r]))
        copies[-1].start()
    for copy in copies:
        copy.wait()


def orthogonal_rows(part, own, other):
    square = pltpu.VMEM((FF, FF), bf16)
    return pl.pallas_call(
        update_kernel,
        in_specs=[VMEM, VMEM, VMEM],
        out_specs=pl.BlockSpec(memory_space=pltpu.HBM),
        out_shape=pltpu.HBM(part.shape, bf16),
        scratch_shapes=[
            pltpu.VMEM((FF, FF), f32),
            square,
            square,
            square,
            square,
            square,
            pltpu.VMEM(part.shape, bf16),
            pltpu.SemaphoreType.DMA((UPDATE_STRIPS,)),
        ],
        compiler_params=pltpu.CompilerParams(vmem_limit_bytes=32 << 20),
        name="orthogonal_rows",
        cost_estimate=pl.CostEstimate(flops=60_000_000_000, bytes_accessed=6_000_000, transcendentals=0),
    )(part, own, other)


def swap(x, axis):
    return lax.ppermute(x, axis, [(0, 1), (1, 0)])


def local(momentum, gradient, owners):
    matrix_count = momentum.shape[0]
    row_count = momentum.shape[1]
    half = matrix_count // 2

    everyone = lax.axis_size(AXES)
    entry_count = float(everyone * gradient.size)
    squares = lax.all_to_all(local_squares(gradient, everyone), AXES, 0, 0, tiled=True)

    def gather(part):
        rows = lax.all_to_all(part, HALF, 0, 0, tiled=True)
        return rows.reshape(HALF_SIZE * row_count, FF)

    def scatter(update):
        return lax.all_to_all(update.reshape(HALF_SIZE, row_count, FF), HALF, 0, 0, tiled=True)

    first = gather(first_step(squares, momentum, gradient, entry_count))
    new_momentum, second, sums = whole_step(squares, momentum, gradient, entry_count)
    sums = sums + swap(sums, "core")
    sums = sums + swap(sums, "near")
    first, sums = lax.optimization_barrier((first, sums))
    own_first = partial_gram(first, sums)
    second, own_first = lax.optimization_barrier((second, own_first))
    other_first = swap(own_first, "far")
    rows = gather(second)
    both = own_first[TAIL + 6 : TAIL + 9].astype(f32) + other_first[TAIL + 6 : TAIL + 9].astype(f32)
    sums = jnp.sum(both, axis=0, keepdims=True)
    first = orthogonal_rows(first, own_first, other_first)
    rows, first = lax.optimization_barrier((rows, first))
    own_second = partial_gram(rows, sums)
    other_second = swap(own_second, "far")
    first, own_second = lax.optimization_barrier((first, own_second))
    first = scatter(first)
    second = scatter(orthogonal_rows(rows, own_second, other_second))
    updates = place(first, 0, matrix_count)
    updates, sums = lax.optimization_barrier((updates, sums))
    around = [lax.ppermute(sums, "y", [(i, (i + k) % 4) for i in range(4)]) for k in range(1, 4)]
    sums = functools.reduce(jnp.add, around, sums)
    updates = place(second, half, matrix_count, updates)

    mine = owners[0] == lax.axis_index(ROW)
    norm = jnp.sqrt(jnp.sum(jnp.where(mine, sums[0, :matrix_count], 0.0)))
    return (new_momentum, updates, (norm / math.sqrt(D * FF)).reshape(1, 1))


def solution(mesh):
    torus = Mesh(mesh.devices.reshape(SIZES), AXES)
    in_specs = (P(EXPERT, ROW, None), P(EXPERT, ROW, None), P(EXPERT, None))
    out_specs = (P(EXPERT, ROW, None), P(EXPERT, ROW, None), P(EXPERT, ROW))
    return jax.shard_map(local, mesh=torus, in_specs=in_specs, out_specs=out_specs, check_vma=False)
```

```python
import functools
import math

import jax
import jax.numpy as jnp
from jax import lax
from jax.experimental import pallas as pl
from jax.experimental.pallas import tpu as pltpu
from jax.sharding import Mesh
from jax.sharding import PartitionSpec as P

D = 2048
FF = 768
AXES = ("zh", "x", "y", "far", "near", "core")
SIZES = (2, 4, 4, 2, 2, 2)
EXPERT = ("zh", "x")
ROW = ("y", "far", "near", "core")
HALF = ("y", "near", "core")
HALF_SIZE = 16

quintic_one = 3.4445
quintic_two = -4.775
quintic_three = 2.0315
momentum_beta = 0.95
clip_rms = 0.25

B = 128
NB = FF // B
OFF = [(i, j) for i in range(NB) for j in range(i + 1, NB)]
PAIRS = [(i, i + 1) for i in range(0, NB, 2)]
TAIL = (len(OFF) + len(PAIRS)) * B
PACKED = TAIL + 16
UPDATE_STRIPS = 4
f32 = jnp.float32
bf16 = jnp.bfloat16
VMEM = pl.BlockSpec(memory_space=pltpu.VMEM)


def square_kernel(g_ref, out_ref, acc):
    step = pl.program_id(0)

    @pl.when(step == 0)
    def _():
        acc[...] = jnp.zeros_like(acc)

    def body(k, total):
        values = g_ref[k].astype(f32)
        return total + jnp.sum((values * values).reshape(-1, 8, FF), axis=0)

    acc[...] = lax.fori_loop(0, g_ref.shape[0], body, acc[...])

    @pl.when(step == pl.num_programs(0) - 1)
    def _():
        total = acc[:, 0:B]
        for j in range(1, NB):
            total = total + acc[:, j * B : (j + 1) * B]
        total = jnp.sum(total, axis=0, keepdims=True)
        out_ref[...] = jnp.broadcast_to(total[None], out_ref.shape)


def local_squares(gradient, copies):
    count = gradient.shape[0]
    return pl.pallas_call(
        square_kernel,
        grid=(4,),
        in_specs=[pl.BlockSpec((count // 4,) + gradient.shape[1:], lambda i: (i, 0, 0))],
        out_specs=pl.BlockSpec((copies, 1, B), lambda i: (0, 0, 0)),
        out_shape=jax.ShapeDtypeStruct((copies, 1, B), f32),
        scratch_shapes=[pltpu.VMEM((8, FF), f32)],
        compiler_params=pltpu.CompilerParams(vmem_limit_bytes=16 << 20),
        name="local_squares",
    )(gradient)


def clip_factor(squares_ref, entry_count):
    total = jnp.sum(squares_ref[:, 0, :], axis=0, keepdims=True)
    total = jnp.sum(total, axis=1, keepdims=True)
    return jnp.minimum(f32(1.0), clip_rms / jnp.sqrt(total / entry_count + 1e-06))


STEP = 4


def step_kernel(entry_count, squares_ref, m_ref, g_ref, out_ref, new_ref, sems):
    factor = clip_factor(squares_ref, entry_count)
    copies = []
    for i in range(new_ref.shape[0] // STEP):
        for k in range(i * STEP, (i + 1) * STEP):
            new = momentum_beta * m_ref[k].astype(f32) + factor * g_ref[k].astype(f32)
            new_ref[k] = new.astype(bf16)
        part = pl.ds(i * STEP, STEP)
        copies.append(pltpu.make_async_copy(new_ref.at[part], out_ref.at[part], sems.at[i]))
        copies[-1].start()
    for copy in copies:
        copy.wait()


def first_step(squares, momentum, gradient, entry_count):
    shape = (momentum.shape[0] // 2,) + momentum.shape[1:]
    return pl.pallas_call(
        functools.partial(step_kernel, entry_count),
        in_specs=[VMEM, VMEM, VMEM],
        out_specs=pl.BlockSpec(memory_space=pltpu.HBM),
        out_shape=pltpu.HBM(shape, bf16),
        scratch_shapes=[pltpu.VMEM(shape, bf16), pltpu.SemaphoreType.DMA((shape[0] // STEP,))],
        compiler_params=pltpu.CompilerParams(vmem_limit_bytes=16 << 20),
        name="first_step",
    )(squares, momentum, gradient)


def whole_step_kernel(entry_count, squares_ref, m_ref, g_ref, new_ref, second_ref, sums_ref):
    step = pl.program_id(0)
    factor = clip_factor(squares_ref, entry_count)
    lanes = lax.broadcasted_iota(jnp.int32, (1, B), 1)

    @pl.when(step == 0)
    def _():
        sums_ref[...] = jnp.zeros_like(sums_ref)

    sums = sums_ref[...]
    for k in range(m_ref.shape[0]):
        new = momentum_beta * m_ref[k].astype(f32) + factor * g_ref[k].astype(f32)
        new = new.astype(bf16)
        new_ref[k] = new
        second_ref[k] = new
        values = new.astype(f32)
        part = jnp.sum((values * values).reshape(-1, 8, FF), axis=0)
        part = jnp.sum(jnp.sum(part, axis=0, keepdims=True), axis=1, keepdims=True)
        sums = sums + jnp.where(lanes == step * STEP + k, part, 0.0)
    sums_ref[...] = sums


def whole_step(squares, momentum, gradient, entry_count):
    count = momentum.shape[0]
    first = count // 2 // STEP
    block = pl.BlockSpec((STEP,) + momentum.shape[1:], lambda i: (i, 0, 0))
    second = pl.BlockSpec((STEP,) + momentum.shape[1:], lambda i: (jnp.maximum(i - first, 0), 0, 0))
    return pl.pallas_call(
        functools.partial(whole_step_kernel, entry_count),
        grid=(count // STEP,),
        in_specs=[pl.BlockSpec(squares.shape, lambda i: (0, 0, 0)), block, block],
        out_specs=[block, second, pl.BlockSpec((1, B), lambda i: (0, 0))],
        out_shape=[
            jax.ShapeDtypeStruct(momentum.shape, bf16),
            pltpu.HBM((count // 2,) + momentum.shape[1:], bf16),
            jax.ShapeDtypeStruct((1, B), f32),
        ],
        compiler_params=pltpu.CompilerParams(vmem_limit_bytes=52 << 20),
        name="whole_step",
    )(squares, momentum, gradient)


def place_kernel(offset, part_ref, *refs):
    out_ref, sems = refs[-2:]
    copies = []
    for i in range(part_ref.shape[0] // STEP):
        source = part_ref.at[pl.ds(i * STEP, STEP)]
        target = out_ref.at[pl.ds(offset + i * STEP, STEP)]
        copies.append(pltpu.make_async_copy(source, target, sems.at[i]))
        copies[-1].start()
    for copy in copies:
        copy.wait()


def place(part, offset, count, into=None):
    operands = [part] if into is None else [part, into]
    return pl.pallas_call(
        functools.partial(place_kernel, offset),
        in_specs=[pl.BlockSpec(memory_space=pl.ANY)] * len(operands),
        out_specs=pl.BlockSpec(memory_space=pltpu.HBM),
        out_shape=pltpu.HBM((count,) + part.shape[1:], bf16),
        scratch_shapes=[pltpu.SemaphoreType.DMA((part.shape[0] // STEP,))],
        input_output_aliases={} if into is None else {1: 0},
        compiler_params=pltpu.CompilerParams(vmem_limit_bytes=16 << 20),
        name="place",
    )(*operands)


def rows_cols():
    return (
        lax.broadcasted_iota(jnp.int32, (B, B), 0),
        lax.broadcasted_iota(jnp.int32, (B, B), 1),
    )


def three_parts(value):
    high = value.astype(bf16).astype(f32)
    middle = (value - high).astype(bf16).astype(f32)
    return [high, middle, value - high - middle]


def gram_kernel(m_ref, sums_ref, packed_ref, gram_ref):
    rows, cols = rows_cols()
    for i in range(3):
        lo = i * 256
        gram_ref[lo : lo + 256, lo:] = lax.dot_general(
            m_ref[:, lo : lo + 256], m_ref[:, lo:], (((0,), (0,)), ((), ())), preferred_element_type=f32
        )

    def block(i, j):
        return gram_ref[i * B : (i + 1) * B, j * B : (j + 1) * B]

    for k, (i, j) in enumerate(OFF):
        packed_ref[k * B : (k + 1) * B, :] = block(i, j).astype(bf16)
    diagonals = []
    squares = None
    for k, (i, j) in enumerate(PAIRS):
        first, second = block(i, i), block(j, j)
        lo = (len(OFF) + k) * B
        packed_ref[lo : lo + B, :] = jnp.where(rows <= cols, first, second).astype(bf16)
        diagonal = jnp.sum(jnp.where(rows == cols, second, 0.0), axis=0, keepdims=True)
        both = jnp.sum(jnp.where(rows == cols, first, 0.0), axis=0, keepdims=True) + diagonal
        diagonals.append(diagonal)
        squares = both if squares is None else squares + both
    tail_rows = diagonals + three_parts(squares) + three_parts(sums_ref[...])
    place = lax.broadcasted_iota(jnp.int32, (16, B), 0)
    tail = jnp.zeros((16, B), f32)
    for r, row in enumerate(tail_rows):
        tail = jnp.where(place == r, jnp.broadcast_to(row, (16, B)), tail)
    packed_ref[TAIL:, :] = tail.astype(bf16)


def partial_gram(part, sums):
    return pl.pallas_call(
        gram_kernel,
        in_specs=[VMEM, VMEM],
        out_specs=VMEM,
        out_shape=jax.ShapeDtypeStruct((PACKED, B), bf16),
        scratch_shapes=[pltpu.VMEM((FF, FF), f32)],
        compiler_params=pltpu.CompilerParams(vmem_limit_bytes=16 << 20),
        name="partial_gram",
        cost_estimate=pl.CostEstimate(flops=2 * part.shape[0] * FF * FF, bytes_accessed=2_000_000, transcendentals=0),
    )(part, sums)


def update_kernel(m_ref, own_ref, other_ref, out_ref, gf, gb, pb, g1b, p1b, qb, u_ref, sems):
    rows, cols = rows_cols()

    def summed(lo, size):
        return own_ref[lo : lo + size, :].astype(f32) + other_ref[lo : lo + size, :].astype(f32)

    tail = summed(TAIL, 16)
    squares = jnp.sum(tail[3:6, :], axis=0, keepdims=True)
    frobenius = jnp.sqrt(jnp.sum(squares, axis=1, keepdims=True))
    scale = 1.0 / (frobenius + 1e-07)
    scale2 = scale * scale

    def put(i, j, value):
        gf[i * B : (i + 1) * B, j * B : (j + 1) * B] = value
        gb[i * B : (i + 1) * B, j * B : (j + 1) * B] = value.astype(bf16)

    for k, (i, j) in enumerate(OFF):
        value = summed(k * B, B) * scale2
        put(i, j, value)
        put(j, i, value.T)
    for k, (i, j) in enumerate(PAIRS):
        merged = summed((len(OFF) + k) * B, B) * scale2
        turned = merged.T
        put(i, i, jnp.where(rows <= cols, merged, turned))
        second = jnp.where(rows > cols, merged, turned)
        put(j, j, jnp.where(rows == cols, jnp.broadcast_to(tail[k : k + 1, :] * scale2, (B, B)), second))

    a, b, c = quintic_one, quintic_two, quintic_three
    strips = [slice(i * 256, (i + 1) * 256) for i in range(3)]
    for s in strips:
        square = jnp.dot(gb[s, :], gb[...], preferred_element_type=f32)
        pb[s, :] = (b * gf[s, :] + c * square).astype(bf16)
    for s in strips:
        gp = jnp.dot(gb[s, :], pb[...], preferred_element_type=f32)
        pgp = jnp.dot(gp.astype(bf16), pb[...], preferred_element_type=f32)
        g1b[s, :] = (a * a * gf[s, :] + 2.0 * a * gp + pgp).astype(bf16)
    for s in strips:
        square = jnp.dot(g1b[s, :], g1b[...], preferred_element_type=f32)
        p1b[s, :] = (b * g1b[s, :].astype(f32) + c * square).astype(bf16)
    for s in strips:
        product = jnp.dot(pb[s, :], p1b[...], preferred_element_type=f32)
        qb[s, :] = (a * (pb[s, :].astype(f32) + p1b[s, :].astype(f32)) + product).astype(bf16)
    last = scale * math.sqrt(D)
    copies = []
    for r in range(UPDATE_STRIPS):
        s = pl.ds(r * 256, 256)
        product = jnp.dot(m_ref[s, :], qb[...], preferred_element_type=f32)
        u_ref[s, :] = ((a * a * m_ref[s, :].astype(f32) + product) * last).astype(bf16)
        copies.append(pltpu.make_async_copy(u_ref.at[s, :], out_ref.at[s, :], sems.at[r]))
        copies[-1].start()
    for copy in copies:
        copy.wait()


def orthogonal_rows(part, own, other):
    square = pltpu.VMEM((FF, FF), bf16)
    return pl.pallas_call(
        update_kernel,
        in_specs=[VMEM, VMEM, VMEM],
        out_specs=pl.BlockSpec(memory_space=pltpu.HBM),
        out_shape=pltpu.HBM(part.shape, bf16),
        scratch_shapes=[
            pltpu.VMEM((FF, FF), f32),
            square,
            square,
            square,
            square,
            square,
            pltpu.VMEM(part.shape, bf16),
            pltpu.SemaphoreType.DMA((UPDATE_STRIPS,)),
        ],
        compiler_params=pltpu.CompilerParams(vmem_limit_bytes=20 << 20),
        name="orthogonal_rows",
        cost_estimate=pl.CostEstimate(flops=60_000_000_000, bytes_accessed=6_000_000, transcendentals=0),
    )(part, own, other)


def swap(x, axis):
    return lax.ppermute(x, axis, [(0, 1), (1, 0)])


def local(momentum, gradient, owners):
    matrix_count = momentum.shape[0]
    row_count = momentum.shape[1]
    half = matrix_count // 2

    everyone = lax.axis_size(AXES)
    entry_count = float(everyone * gradient.size)
    squares = lax.all_to_all(local_squares(gradient, everyone), AXES, 0, 0, tiled=True)

    def gather(part):
        rows = lax.all_to_all(part, HALF, 0, 0, tiled=True)
        return rows.reshape(HALF_SIZE * row_count, FF)

    def scatter(update):
        return lax.all_to_all(update.reshape(HALF_SIZE, row_count, FF), HALF, 0, 0, tiled=True)

    first = gather(first_step(squares, momentum, gradient, entry_count))
    new_momentum, second, sums = whole_step(squares, momentum, gradient, entry_count)
    sums = sums + swap(sums, "core")
    sums = sums + swap(sums, "near")
    first, sums = lax.optimization_barrier((first, sums))
    own_first = partial_gram(first, sums)
    second, own_first = lax.optimization_barrier((second, own_first))
    other_first = swap(own_first, "far")
    rows = gather(second)
    both = own_first[TAIL + 6 : TAIL + 9].astype(f32) + other_first[TAIL + 6 : TAIL + 9].astype(f32)
    sums = jnp.sum(both, axis=0, keepdims=True)
    first = orthogonal_rows(first, own_first, other_first)
    rows, first = lax.optimization_barrier((rows, first))
    own_second = partial_gram(rows, sums)
    other_second = swap(own_second, "far")
    first, own_second = lax.optimization_barrier((first, own_second))
    first = scatter(first)
    second = scatter(orthogonal_rows(rows, own_second, other_second))
    updates = place(first, 0, matrix_count)
    updates, sums = lax.optimization_barrier((updates, sums))
    around = [lax.ppermute(sums, "y", [(i, (i + k) % 4) for i in range(4)]) for k in range(1, 4)]
    sums = functools.reduce(jnp.add, around, sums)
    updates = place(second, half, matrix_count, updates)

    mine = owners[0] == lax.axis_index(ROW)
    norm = jnp.sqrt(jnp.sum(jnp.where(mine, sums[0, :matrix_count], 0.0)))
    return (new_momentum, updates, (norm / math.sqrt(D * FF)).reshape(1, 1))


def solution(mesh):
    torus = Mesh(mesh.devices.reshape(SIZES), AXES)
    in_specs = (P(EXPERT, ROW, None), P(EXPERT, ROW, None), P(EXPERT, None))
    out_specs = (P(EXPERT, ROW, None), P(EXPERT, ROW, None), P(EXPERT, ROW))
    return jax.shard_map(local, mesh=torus, in_specs=in_specs, out_specs=out_specs, check_vma=False)
```

```python
import functools
import math

import jax
import jax.numpy as jnp
from jax import lax
from jax.experimental import pallas as pl
from jax.experimental.pallas import tpu as pltpu
from jax.sharding import Mesh
from jax.sharding import PartitionSpec as P

D = 2048
FF = 768
AXES = ("zh", "x", "y", "far", "near", "core")
SIZES = (2, 4, 4, 2, 2, 2)
EXPERT = ("zh", "x")
ROW = ("y", "far", "near", "core")
HALF = ("y", "near", "core")
HALF_SIZE = 16

quintic_one = 3.4445
quintic_two = -4.775
quintic_three = 2.0315
momentum_beta = 0.95
clip_rms = 0.25

B = 128
NB = FF // B
OFF = [(i, j) for i in range(NB) for j in range(i + 1, NB)]
PAIRS = [(i, i + 1) for i in range(0, NB, 2)]
TAIL = (len(OFF) + len(PAIRS)) * B
PACKED = TAIL + 16
UPDATE_STRIPS = 4
f32 = jnp.float32
bf16 = jnp.bfloat16
VMEM = pl.BlockSpec(memory_space=pltpu.VMEM)


def square_kernel(g_ref, out_ref):
    def body(k, total):
        values = g_ref[k].astype(f32)
        return total + jnp.sum((values * values).reshape(-1, 8, FF), axis=0)

    acc = lax.fori_loop(0, g_ref.shape[0], body, jnp.zeros((8, FF), f32))
    total = acc[:, 0:B]
    for j in range(1, NB):
        total = total + acc[:, j * B : (j + 1) * B]
    total = jnp.sum(total, axis=0, keepdims=True)
    out_ref[...] = jnp.broadcast_to(total[None], out_ref.shape)


def local_squares(gradient, copies):
    return pl.pallas_call(
        square_kernel,
        in_specs=[VMEM],
        out_specs=VMEM,
        out_shape=jax.ShapeDtypeStruct((copies, 1, B), f32),
        compiler_params=pltpu.CompilerParams(vmem_limit_bytes=16 << 20),
        name="local_squares",
    )(gradient)


def clip_factor(squares_ref, entry_count):
    total = jnp.sum(squares_ref[:, 0, :], axis=0, keepdims=True)
    total = jnp.sum(total, axis=1, keepdims=True)
    return jnp.minimum(f32(1.0), clip_rms / jnp.sqrt(total / entry_count + 1e-06))


STEP = 4


def step_kernel(entry_count, squares_ref, m_ref, g_ref, out_ref, new_ref, sems):
    factor = clip_factor(squares_ref, entry_count)
    copies = []
    for i in range(new_ref.shape[0] // STEP):
        for k in range(i * STEP, (i + 1) * STEP):
            new = momentum_beta * m_ref[k].astype(f32) + factor * g_ref[k].astype(f32)
            new_ref[k] = new.astype(bf16)
        part = pl.ds(i * STEP, STEP)
        copies.append(pltpu.make_async_copy(new_ref.at[part], out_ref.at[part], sems.at[i]))
        copies[-1].start()
    for copy in copies:
        copy.wait()


def first_step(squares, momentum, gradient, entry_count):
    shape = (momentum.shape[0] // 2,) + momentum.shape[1:]
    return pl.pallas_call(
        functools.partial(step_kernel, entry_count),
        in_specs=[VMEM, VMEM, VMEM],
        out_specs=pl.BlockSpec(memory_space=pltpu.HBM),
        out_shape=pltpu.HBM(shape, bf16),
        scratch_shapes=[pltpu.VMEM(shape, bf16), pltpu.SemaphoreType.DMA((shape[0] // STEP,))],
        compiler_params=pltpu.CompilerParams(vmem_limit_bytes=16 << 20),
        name="first_step",
    )(squares, momentum, gradient)


def whole_step_kernel(entry_count, squares_ref, m_ref, g_ref, new_ref, second_ref, sums_ref):
    step = pl.program_id(0)
    factor = clip_factor(squares_ref, entry_count)
    lanes = lax.broadcasted_iota(jnp.int32, (1, B), 1)

    @pl.when(step == 0)
    def _():
        sums_ref[...] = jnp.zeros_like(sums_ref)

    sums = sums_ref[...]
    for k in range(m_ref.shape[0]):
        new = momentum_beta * m_ref[k].astype(f32) + factor * g_ref[k].astype(f32)
        new = new.astype(bf16)
        new_ref[k] = new
        second_ref[k] = new
        values = new.astype(f32)
        part = jnp.sum((values * values).reshape(-1, 8, FF), axis=0)
        part = jnp.sum(jnp.sum(part, axis=0, keepdims=True), axis=1, keepdims=True)
        sums = sums + jnp.where(lanes == step * STEP + k, part, 0.0)
    sums_ref[...] = sums


def whole_step(squares, momentum, gradient, entry_count):
    count = momentum.shape[0]
    first = count // 2 // STEP
    block = pl.BlockSpec((STEP,) + momentum.shape[1:], lambda i: (i, 0, 0))
    second = pl.BlockSpec((STEP,) + momentum.shape[1:], lambda i: (jnp.maximum(i - first, 0), 0, 0))
    return pl.pallas_call(
        functools.partial(whole_step_kernel, entry_count),
        grid=(count // STEP,),
        in_specs=[pl.BlockSpec(squares.shape, lambda i: (0, 0, 0)), block, block],
        out_specs=[block, second, pl.BlockSpec((1, B), lambda i: (0, 0))],
        out_shape=[
            jax.ShapeDtypeStruct(momentum.shape, bf16),
            pltpu.HBM((count // 2,) + momentum.shape[1:], bf16),
            jax.ShapeDtypeStruct((1, B), f32),
        ],
        compiler_params=pltpu.CompilerParams(vmem_limit_bytes=52 << 20),
        name="whole_step",
    )(squares, momentum, gradient)


def place_kernel(offset, part_ref, *refs):
    out_ref, sems = refs[-2:]
    copies = []
    for i in range(part_ref.shape[0] // STEP):
        source = part_ref.at[pl.ds(i * STEP, STEP)]
        target = out_ref.at[pl.ds(offset + i * STEP, STEP)]
        copies.append(pltpu.make_async_copy(source, target, sems.at[i]))
        copies[-1].start()
    for copy in copies:
        copy.wait()


def place(part, offset, count, into=None):
    operands = [part] if into is None else [part, into]
    return pl.pallas_call(
        functools.partial(place_kernel, offset),
        in_specs=[pl.BlockSpec(memory_space=pl.ANY)] * len(operands),
        out_specs=pl.BlockSpec(memory_space=pltpu.HBM),
        out_shape=pltpu.HBM((count,) + part.shape[1:], bf16),
        scratch_shapes=[pltpu.SemaphoreType.DMA((part.shape[0] // STEP,))],
        input_output_aliases={} if into is None else {1: 0},
        compiler_params=pltpu.CompilerParams(vmem_limit_bytes=16 << 20),
        name="place",
    )(*operands)


def rows_cols():
    return (
        lax.broadcasted_iota(jnp.int32, (B, B), 0),
        lax.broadcasted_iota(jnp.int32, (B, B), 1),
    )


def three_parts(value):
    high = value.astype(bf16).astype(f32)
    middle = (value - high).astype(bf16).astype(f32)
    return [high, middle, value - high - middle]


def gram_kernel(m_ref, sums_ref, packed_ref, gram_ref):
    rows, cols = rows_cols()
    for i in range(3):
        lo = i * 256
        gram_ref[lo : lo + 256, lo:] = lax.dot_general(
            m_ref[:, lo : lo + 256], m_ref[:, lo:], (((0,), (0,)), ((), ())), preferred_element_type=f32
        )

    def block(i, j):
        return gram_ref[i * B : (i + 1) * B, j * B : (j + 1) * B]

    for k, (i, j) in enumerate(OFF):
        packed_ref[k * B : (k + 1) * B, :] = block(i, j).astype(bf16)
    diagonals = []
    squares = None
    for k, (i, j) in enumerate(PAIRS):
        first, second = block(i, i), block(j, j)
        lo = (len(OFF) + k) * B
        packed_ref[lo : lo + B, :] = jnp.where(rows <= cols, first, second).astype(bf16)
        diagonal = jnp.sum(jnp.where(rows == cols, second, 0.0), axis=0, keepdims=True)
        both = jnp.sum(jnp.where(rows == cols, first, 0.0), axis=0, keepdims=True) + diagonal
        diagonals.append(diagonal)
        squares = both if squares is None else squares + both
    tail_rows = diagonals + three_parts(squares) + three_parts(sums_ref[...])
    place = lax.broadcasted_iota(jnp.int32, (16, B), 0)
    tail = jnp.zeros((16, B), f32)
    for r, row in enumerate(tail_rows):
        tail = jnp.where(place == r, jnp.broadcast_to(row, (16, B)), tail)
    packed_ref[TAIL:, :] = tail.astype(bf16)


def partial_gram(part, sums):
    return pl.pallas_call(
        gram_kernel,
        in_specs=[VMEM, VMEM],
        out_specs=VMEM,
        out_shape=jax.ShapeDtypeStruct((PACKED, B), bf16),
        scratch_shapes=[pltpu.VMEM((FF, FF), f32)],
        compiler_params=pltpu.CompilerParams(vmem_limit_bytes=24 << 20),
        name="partial_gram",
        cost_estimate=pl.CostEstimate(flops=2 * part.shape[0] * FF * FF, bytes_accessed=2_000_000, transcendentals=0),
    )(part, sums)


def update_kernel(m_ref, own_ref, other_ref, out_ref, gf, gb, pb, g1b, p1b, qb, u_ref, sems):
    rows, cols = rows_cols()

    def summed(lo, size):
        return own_ref[lo : lo + size, :].astype(f32) + other_ref[lo : lo + size, :].astype(f32)

    tail = summed(TAIL, 16)
    squares = jnp.sum(tail[3:6, :], axis=0, keepdims=True)
    frobenius = jnp.sqrt(jnp.sum(squares, axis=1, keepdims=True))
    scale = 1.0 / (frobenius + 1e-07)
    scale2 = scale * scale

    def put(i, j, value):
        gf[i * B : (i + 1) * B, j * B : (j + 1) * B] = value
        gb[i * B : (i + 1) * B, j * B : (j + 1) * B] = value.astype(bf16)

    for k, (i, j) in enumerate(OFF):
        value = summed(k * B, B) * scale2
        put(i, j, value)
        put(j, i, value.T)
    for k, (i, j) in enumerate(PAIRS):
        merged = summed((len(OFF) + k) * B, B) * scale2
        turned = merged.T
        put(i, i, jnp.where(rows <= cols, merged, turned))
        second = jnp.where(rows > cols, merged, turned)
        put(j, j, jnp.where(rows == cols, jnp.broadcast_to(tail[k : k + 1, :] * scale2, (B, B)), second))

    a, b, c = quintic_one, quintic_two, quintic_three
    strips = [slice(i * 256, (i + 1) * 256) for i in range(3)]
    for s in strips:
        square = jnp.dot(gb[s, :], gb[...], preferred_element_type=f32)
        pb[s, :] = (b * gf[s, :] + c * square).astype(bf16)
    for s in strips:
        gp = jnp.dot(gb[s, :], pb[...], preferred_element_type=f32)
        pgp = jnp.dot(gp.astype(bf16), pb[...], preferred_element_type=f32)
        g1b[s, :] = (a * a * gf[s, :] + 2.0 * a * gp + pgp).astype(bf16)
    for s in strips:
        square = jnp.dot(g1b[s, :], g1b[...], preferred_element_type=f32)
        p1b[s, :] = (b * g1b[s, :].astype(f32) + c * square).astype(bf16)
    for s in strips:
        product = jnp.dot(pb[s, :], p1b[...], preferred_element_type=f32)
        qb[s, :] = (a * (pb[s, :].astype(f32) + p1b[s, :].astype(f32)) + product).astype(bf16)
    last = scale * math.sqrt(D)
    copies = []
    for r in range(UPDATE_STRIPS):
        s = pl.ds(r * 256, 256)
        product = jnp.dot(m_ref[s, :], qb[...], preferred_element_type=f32)
        u_ref[s, :] = ((a * a * m_ref[s, :].astype(f32) + product) * last).astype(bf16)
        copies.append(pltpu.make_async_copy(u_ref.at[s, :], out_ref.at[s, :], sems.at[r]))
        copies[-1].start()
    for copy in copies:
        copy.wait()


def orthogonal_rows(part, own, other):
    square = pltpu.VMEM((FF, FF), bf16)
    return pl.pallas_call(
        update_kernel,
        in_specs=[VMEM, VMEM, VMEM],
        out_specs=pl.BlockSpec(memory_space=pltpu.HBM),
        out_shape=pltpu.HBM(part.shape, bf16),
        scratch_shapes=[
            pltpu.VMEM((FF, FF), f32),
            square,
            square,
            square,
            square,
            square,
            pltpu.VMEM(part.shape, bf16),
            pltpu.SemaphoreType.DMA((UPDATE_STRIPS,)),
        ],
        compiler_params=pltpu.CompilerParams(vmem_limit_bytes=32 << 20),
        name="orthogonal_rows",
        cost_estimate=pl.CostEstimate(flops=60_000_000_000, bytes_accessed=6_000_000, transcendentals=0),
    )(part, own, other)


def swap(x, axis):
    return lax.ppermute(x, axis, [(0, 1), (1, 0)])


def local(momentum, gradient, owners):
    matrix_count = momentum.shape[0]
    row_count = momentum.shape[1]
    half = matrix_count // 2

    everyone = lax.axis_size(AXES)
    entry_count = float(everyone * gradient.size)
    squares = lax.all_to_all(local_squares(gradient, everyone), AXES, 0, 0, tiled=True)

    def gather(part):
        rows = lax.all_to_all(part, HALF, 0, 0, tiled=True)
        return rows.reshape(HALF_SIZE * row_count, FF)

    def scatter(update):
        return lax.all_to_all(update.reshape(HALF_SIZE, row_count, FF), HALF, 0, 0, tiled=True)

    first = gather(first_step(squares, momentum, gradient, entry_count))
    new_momentum, second, sums = whole_step(squares, momentum, gradient, entry_count)
    sums = sums + swap(sums, "core")
    sums = sums + swap(sums, "near")
    first, sums = lax.optimization_barrier((first, sums))
    own_first = partial_gram(first, sums)
    second, own_first = lax.optimization_barrier((second, own_first))
    other_first = swap(own_first, "far")
    rows = gather(second)
    both = own_first[TAIL + 6 : TAIL + 9].astype(f32) + other_first[TAIL + 6 : TAIL + 9].astype(f32)
    sums = jnp.sum(both, axis=0, keepdims=True)
    first = orthogonal_rows(first, own_first, other_first)
    rows, first = lax.optimization_barrier((rows, first))
    own_second = partial_gram(rows, sums)
    other_second = swap(own_second, "far")
    first, own_second = lax.optimization_barrier((first, own_second))
    first = scatter(first)
    second = scatter(orthogonal_rows(rows, own_second, other_second))
    updates = place(first, 0, matrix_count)
    updates, sums = lax.optimization_barrier((updates, sums))
    around = [lax.ppermute(sums, "y", [(i, (i + k) % 4) for i in range(4)]) for k in range(1, 4)]
    sums = functools.reduce(jnp.add, around, sums)
    updates = place(second, half, matrix_count, updates)

    mine = owners[0] == lax.axis_index(ROW)
    norm = jnp.sqrt(jnp.sum(jnp.where(mine, sums[0, :matrix_count], 0.0)))
    return (new_momentum, updates, (norm / math.sqrt(D * FF)).reshape(1, 1))


def solution(mesh):
    torus = Mesh(mesh.devices.reshape(SIZES), AXES)
    in_specs = (P(EXPERT, ROW, None), P(EXPERT, ROW, None), P(EXPERT, None))
    out_specs = (P(EXPERT, ROW, None), P(EXPERT, ROW, None), P(EXPERT, ROW))
    return jax.shard_map(local, mesh=torus, in_specs=in_specs, out_specs=out_specs, check_vma=False)
```
